32 devices in a mesh: grp: 2 (over y), chan: 8 (over z, x), band: 2 (over core).
Axes of the slice: x: 2, y: 2, z: 4, core: 2. Of those that a mesh axis runs over, the one named last changes fastest.
Arguments:
- spectra: float32 [2, 32, 1280, 256], P(None, 'band', ('grp', 'chan')), parts along dimension 2, may hold values from -6 to 6
- channel_order: int32 [16, 80], P(('grp', 'chan')), parts along dimension 0, may hold values from 0 to 79, each once within a row
- bin_assign: int32 [32], replicated, may hold values from 0 to 31, each once
Outputs:
- correlations: float32 [16, 3, 64, 6400], P(('grp', 'chan'), None, None, 'band'), parts along dimension 0
The draws below stay inside these ranges and needn't reach their ends.
There are 2 independent parts, one for each index of `grp`. The reference program is written for one: setup_inputs(seed, part) draws one part's arguments, and reference() takes and returns one part's arrays. A program takes and returns all parts, laid end to end along the dimension named above; an argument that names none is the same for every part. Nothing has to cross between parts.
Inputs may be any that keep to these rules, and one draw needn't show every extreme that they name: `channel_order`: each row is a permutation of 0 .. 79. `bin_assign`: a permutation of 0 .. 31.
All inputs are finite; a program needn't handle non-finite values.
Results may differ from the reference program's by a relative error of at most 0.0003.
Values sent between devices are 32-bit elements; how exact they have to be, the bound alone decides.
A program may use at most 128 MiB of HBM per device.

```python
import math
import jax
import jax.numpy as jnp
from jax import lax

CH_DEV = 80
WIN = 256
BLOCKS = 8
CHANNELS = 640
BINS = 32
N_CHAN = 8


def block_scale(own_key, dims, split, least, largest):
    gain, own = 1.0, jax.random.fold_in(own_key, 6)
    for dim, shards_of in split:
        draws = jnp.exp(jax.random.uniform(jax.random.fold_in(own, dim), (shards_of,), jnp.float32, least / len(split), largest / len(split)))
        gain = gain * jnp.repeat(draws, dims[dim] // shards_of).reshape([-1 if axis == dim else 1 for axis in range(len(dims))])
    return gain


def centred(stream_key, shape, width, most, pieces=(), kind=jnp.bfloat16):
    loudness = block_scale(stream_key, shape, pieces, -0.22, 0.18) if pieces else 1.0
    entries = jax.random.normal(stream_key, shape, jnp.float32) * width * loudness
    return jnp.minimum(jnp.maximum(entries, -most), most).astype(kind)


def setup_inputs(seed: int = 0, part: int = 0) -> dict:
    seeds = jax.random.split(jax.random.key(seed), 4)
    own_keys = jax.random.split(jax.random.fold_in(seeds[3], part), 4)
    spectra = centred(own_keys[0], (2, BINS, CHANNELS, WIN), 1.0, 6.0, ((1, 2), (2, 8)), jnp.float32)
    channel_order = jax.vmap(lambda own: jax.random.permutation(own, CH_DEV))(jax.random.split(own_keys[1], BLOCKS)).reshape((BLOCKS, CH_DEV)).astype(jnp.int32)
    bin_assign = jax.random.permutation(seeds[2], BINS).astype(jnp.int32)
    return {"spectra": spectra, "channel_order": channel_order, "bin_assign": bin_assign}


HIGHEST = lax.Precision.HIGHEST


def cross_spectra(first_block, second_block, factor):
    left_real = jnp.concatenate([first_block[0], first_block[1]], axis=2)
    left_imag = jnp.concatenate([first_block[1], -first_block[0]], axis=2)
    left_both = jnp.stack([left_real, left_imag])
    right_both = jnp.concatenate([second_block[0], second_block[1]], axis=2)
    products = jnp.einsum("rfiw,fjw->rfij", left_both, right_both, precision=HIGHEST)
    bins_here = first_block.shape[1]
    row_count = first_block.shape[2]
    return products.reshape(2, bins_here, row_count * row_count) * factor


def lag_table(bin_assign, lag_count):
    lag_steps = jnp.arange(lag_count, dtype=jnp.int32)
    phase_step = (bin_assign[:, None] * lag_steps[None, :]) % lag_count
    angles = phase_step.astype(jnp.float32) * (2.0 * math.pi / lag_count)
    return jnp.stack([jnp.cos(angles), -jnp.sin(angles)])


def arrange(block_data, row_order):
    return block_data[:, :, row_order, :]


def reference(spectra, channel_order, bin_assign):
    block_count = channel_order.shape[0]
    row_count = channel_order.shape[1]
    grouped = spectra.reshape(2, BINS, block_count, row_count, WIN)
    ordered = jax.vmap(arrange, in_axes=(2, 0), out_axes=2)(grouped, channel_order)
    lag_weights = lag_table(bin_assign, 2 * BINS)
    offsets = (0, N_CHAN // 4, N_CHAN // 2)

    def one_block(block_index):
        local_block = lax.dynamic_index_in_dim(ordered, block_index, 2, keepdims=False)
        results = []
        for offset in offsets:
            partner = lax.dynamic_index_in_dim(ordered, (block_index + offset) % block_count, 2, keepdims=False)
            spectra_pair = cross_spectra(local_block, partner, 1.0 / WIN)
            results.append(jnp.einsum("rsc,rsl->lc", spectra_pair, lag_weights, precision=HIGHEST))
        return jnp.stack(results)

    return lax.map(one_block, jnp.arange(block_count, dtype=jnp.int32))
```

```python
import functools
import math

import jax
import jax.numpy as jnp
from jax import lax
from jax.experimental import pallas as pl
from jax.experimental.pallas import tpu as pltpu
from jax.sharding import PartitionSpec as P

MEMBERS = 4
F32 = jnp.float32
BF16 = jnp.bfloat16
VMEM = pl.BlockSpec(memory_space=pltpu.VMEM)
SMEM = pl.BlockSpec(memory_space=pltpu.SMEM)
LIMIT = 40 * 1024 * 1024


def halves(x):
    high = x.astype(BF16)
    low = (x - high.astype(F32)).astype(BF16)
    return high, low


def thirds(x):
    high = x.astype(BF16)
    rest = x - high.astype(F32)
    middle = rest.astype(BF16)
    low = (rest - middle.astype(F32)).astype(BF16)
    return high, middle, low


def dot(left, right, dims):
    return lax.dot_general(left, right, (dims, ((), ())), preferred_element_type=F32)


def order_kernel(distance, place, order, spectra, ordered):
    parts, bins, rows, _ = ordered.shape
    chunk = lax.rem(place[0] + distance, MEMBERS)
    row_ids = lax.broadcasted_iota(jnp.int32, (rows, rows), 0)
    chosen = jnp.where(row_ids == order[...], 1.0, 0.0).astype(BF16)
    chosen = jnp.concatenate([chosen] * 3, axis=0)
    for part in range(parts):
        for slot in range(bins):
            values = spectra[part, chunk * bins + slot]
            stacked = jnp.concatenate(thirds(values), axis=0)
            ordered[part, slot] = dot(chosen, stacked, ((0,), (0,)))


def ordered_chunk(place, order, spectra, distance):
    parts, bins, rows, windows = spectra.shape
    return pl.pallas_call(
        functools.partial(order_kernel, distance),
        out_shape=jax.ShapeDtypeStruct((parts, bins // MEMBERS, rows, windows), F32),
        in_specs=[SMEM, VMEM, VMEM],
        out_specs=VMEM,
        compiler_params=pltpu.CompilerParams(vmem_limit_bytes=LIMIT),
        name=f"order_{distance}",
    )(place, order, spectra)


def left_operand(real, imag):
    stacked = jnp.concatenate(
        [
            jnp.concatenate([real, imag], axis=1),
            jnp.concatenate([imag, -real], axis=1),
        ],
        axis=0,
    )
    return halves(stacked)


def right_operand(real, imag):
    return halves(jnp.concatenate([real, imag], axis=1))


def product(left, right):
    dims = ((1,), (1,))
    return (
        dot(left[0], right[0], dims)
        + dot(left[0], right[1], dims)
        + dot(left[1], right[0], dims)
    )


def packed_rows(scratch, lead, first, rows, group, count):
    pieces = [
        scratch[lead, pl.ds(first + group * 8 + step, count, stride=rows), :][:, :rows]
        for step in range(8)
    ]
    return jnp.concatenate(pieces, axis=1)


def self_kernel(place, *refs):
    chunks, (same, other), scratch = refs[:MEMBERS], refs[MEMBERS:-1], refs[-1]
    _, bins, rows, _ = chunks[0].shape
    half = rows // 2
    count = 2 * bins
    width = 8 * rows
    for distance in range(MEMBERS):
        chunk = chunks[distance]
        block = (MEMBERS - distance) % MEMBERS
        for slot in range(bins):
            real, imag = chunk[0, slot], chunk[1, slot]
            value = product(left_operand(real, imag), right_operand(real, imag))
            scratch[distance, slot * 2 * rows : (slot + 1) * 2 * rows, 0:rows] = value
        for out, shift in ((same, 0), (other, 1)):
            first = lax.rem(place[1] + shift, 2) * half
            for group in range(half // 8):
                out[block * count : (block + 1) * count, group * width : (group + 1) * width] = (
                    packed_rows(scratch, distance, first, rows, group, count)
                )


def pair_kernel(place, *refs):
    blocks, outs, scratch = refs[:MEMBERS], refs[MEMBERS:-1], refs[-1]
    _, bins, rows, _ = blocks[0].shape
    half = rows // 2
    count = 2 * bins
    width = 8 * rows
    for slot in range(bins):
        rights = []
        lefts = []
        for block in blocks:
            real, imag = block[0, slot], block[1, slot]
            rights.append(right_operand(real, imag))
            lefts.append(left_operand(real, imag))
        for owner in range(MEMBERS):
            for pair in range(2):
                partner = (owner + pair + 1) % MEMBERS
                scratch[owner * 2 + pair, slot * 2 * rows : (slot + 1) * 2 * rows, 0:rows] = (
                    product(lefts[owner], rights[partner])
                )
    for owner in range(MEMBERS):
        for shift in range(2):
            first = lax.rem(place[1] + shift, 2) * half
            for pair in range(2):
                for group in range(half // 8):
                    outs[owner * 2 + shift][pair, :, group * width : (group + 1) * width] = (
                        packed_rows(scratch, owner * 2 + pair, first, rows, group, count)
                    )


def self_pairs(place, chunks):
    _, bins, rows, windows = chunks[0].shape
    columns = rows * rows // 2
    shape = jax.ShapeDtypeStruct((MEMBERS * 2 * bins, columns), F32)
    flops = MEMBERS * bins * 3 * 2 * 4 * rows * rows * windows
    return pl.pallas_call(
        self_kernel,
        out_shape=(shape, shape),
        in_specs=[SMEM] + [VMEM] * MEMBERS,
        out_specs=(VMEM, VMEM),
        scratch_shapes=[pltpu.VMEM((MEMBERS, 2 * bins * rows, 128), F32)],
        compiler_params=pltpu.CompilerParams(vmem_limit_bytes=LIMIT),
        cost_estimate=pl.CostEstimate(flops=flops * 8, bytes_accessed=1 << 22, transcendentals=0),
        name="self_pairs",
    )(place, *chunks)


def partner_pairs(place, blocks):
    _, bins, rows, windows = blocks[0].shape
    columns = rows * rows // 2
    shape = jax.ShapeDtypeStruct((2, 2 * bins, columns), F32)
    flops = 2 * MEMBERS * bins * 3 * 2 * 4 * rows * rows * windows
    return pl.pallas_call(
        pair_kernel,
        out_shape=(shape,) * (2 * MEMBERS),
        in_specs=[SMEM] + [VMEM] * MEMBERS,
        out_specs=(VMEM,) * (2 * MEMBERS),
        scratch_shapes=[pltpu.VMEM((2 * MEMBERS, 2 * bins * rows, 128), F32)],
        compiler_params=pltpu.CompilerParams(vmem_limit_bytes=LIMIT),
        cost_estimate=pl.CostEstimate(flops=flops, bytes_accessed=1 << 22, transcendentals=0),
        name="partner_pairs",
    )(place, *blocks)


def lag_kernel(table, same, other, *refs):
    pieces, out = refs[:-1], refs[-1]
    columns = out.shape[2]
    tile = 640 if columns % 640 == 0 else columns
    high, low = halves(table[...])
    dims = ((1,), (0,))
    for pair in range(3):
        for at in range(0, columns, tile):
            span = slice(at, at + tile)
            if pair == 0:
                stacked = jnp.concatenate([same[:, span], other[:, span]], axis=0)
            else:
                stacked = jnp.concatenate([piece[pair - 1, :, span] for piece in pieces], axis=0)
            first, second = halves(stacked)
            out[pair, :, span] = dot(high, first, dims) + dot(high, second, dims) + dot(low, first, dims)


def lag_transform(table, same, other, pieces):
    lags = table.shape[0]
    columns = same.shape[1]
    return pl.pallas_call(
        lag_kernel,
        out_shape=jax.ShapeDtypeStruct((3, lags, columns), F32),
        in_specs=[VMEM] * (3 + len(pieces)),
        out_specs=VMEM,
        compiler_params=pltpu.CompilerParams(vmem_limit_bytes=LIMIT),
        name="lag_transform",
    )(table, same, other, *pieces)


def lag_table(bin_assign, member, band, factor):
    bins = bin_assign.shape[0]
    lags = 2 * bins
    chunk = bins // (2 * MEMBERS)
    column = jnp.arange(lags, dtype=jnp.int32)
    shift = column // (MEMBERS * 2 * chunk)
    distance = column // (2 * chunk) % MEMBERS
    slot = column // 2 % chunk
    part = column % 2
    where = (band + shift) % 2 * (MEMBERS * chunk) + (member - distance + MEMBERS) % MEMBERS * chunk + slot
    steps = jnp.arange(lags, dtype=jnp.int32)
    phase = steps[:, None] * bin_assign[where][None, :] % lags
    angles = phase.astype(F32) * (2.0 * math.pi / lags)
    return jnp.where(part[None, :] == 0, jnp.cos(angles), -jnp.sin(angles)) * factor


def on_device(loop_size, spectra, channel_order, bin_assign):
    quarter = loop_size // MEMBERS
    chan = lax.axis_index("chan")
    band = lax.axis_index("band")
    member = chan // quarter
    place = jnp.stack([member, band]).astype(jnp.int32)
    blocks = [None] * MEMBERS
    chunks = [None] * MEMBERS
    for distance in (2, 3, 1, 0):
        chunk = ordered_chunk(place, channel_order, spectra, distance)
        chunks[distance] = chunk
        if distance:
            route = [(i, (i + distance * quarter) % loop_size) for i in range(loop_size)]
            blocks[MEMBERS - distance] = lax.ppermute(chunk, "chan", route)
        else:
            blocks[0] = chunk
    same, other = self_pairs(place, chunks)
    other = lax.ppermute(other, "band", [(0, 1), (1, 0)])
    results = partner_pairs(place, blocks)
    pieces = []
    for shift in range(2):
        for distance in range(MEMBERS):
            piece = results[distance * 2 + shift]
            if distance or shift:
                route = [
                    (i * 2 + j, (i + distance * quarter) % loop_size * 2 + (j + shift) % 2)
                    for i in range(loop_size)
                    for j in range(2)
                ]
                piece = lax.ppermute(piece, ("chan", "band"), route)
            pieces.append(piece)
    table = lag_table(bin_assign, member, band, 1.0 / spectra.shape[3])
    return lag_transform(table, same, other, pieces)[None]


def solution(mesh):
    in_specs = (P(None, "band", ("grp", "chan"), None), P(("grp", "chan"), None), P())
    out_specs = P(("grp", "chan"), None, None, "band")
    return jax.shard_map(
        functools.partial(on_device, mesh.shape["chan"]),
        mesh=mesh,
        in_specs=in_specs,
        out_specs=out_specs,
        check_vma=False,
    )
```

```python
import functools
import math

import jax
import jax.numpy as jnp
from jax import lax
from jax.experimental import pallas as pl
from jax.experimental.pallas import tpu as pltpu
from jax.sharding import PartitionSpec as P

MEMBERS = 4
F32 = jnp.float32
BF16 = jnp.bfloat16
VMEM = pl.BlockSpec(memory_space=pltpu.VMEM)
SMEM = pl.BlockSpec(memory_space=pltpu.SMEM)
PIECES = [
    (2, 0, (1,)),
    (2, 1, (1,)),
    (2, 0, (0,)),
    (2, 1, (0,)),
    (1, 0, (1,)),
    (1, 1, (1,)),
    (3, 0, (0, 1)),
    (3, 1, (0, 1)),
    (1, 0, (0,)),
    (1, 1, (0,)),
    (0, 1, (0, 1)),
    (0, 0, (0, 1)),
]
LIMIT = 40 * 1024 * 1024


def halves(x):
    high = x.astype(BF16)
    low = (x - high.astype(F32)).astype(BF16)
    return high, low


def thirds(x):
    high = x.astype(BF16)
    rest = x - high.astype(F32)
    middle = rest.astype(BF16)
    low = (rest - middle.astype(F32)).astype(BF16)
    return high, middle, low


def dot(left, right, dims):
    return lax.dot_general(left, right, (dims, ((), ())), preferred_element_type=F32)


def order_kernel(which, place, order, spectra, ordered):
    parts, bins, rows, _ = ordered.shape
    chunk = place[2 + which]
    row_ids = lax.broadcasted_iota(jnp.int32, (rows, rows), 0)
    chosen = jnp.where(row_ids == order[...], 1.0, 0.0).astype(BF16)
    chosen = jnp.concatenate([chosen] * 3, axis=0)
    for part in range(parts):
        for slot in range(bins):
            values = spectra[part, chunk * bins + slot]
            stacked = jnp.concatenate(thirds(values), axis=0)
            ordered[part, slot] = dot(chosen, stacked, ((0,), (0,)))


def ordered_chunk(place, order, spectra, which):
    parts, bins, rows, windows = spectra.shape
    return pl.pallas_call(
        functools.partial(order_kernel, which),
        out_shape=jax.ShapeDtypeStruct((parts, bins // MEMBERS, rows, windows), F32),
        in_specs=[SMEM, VMEM, VMEM],
        out_specs=VMEM,
        compiler_params=pltpu.CompilerParams(vmem_limit_bytes=LIMIT),
        name=f"order_{which}",
    )(place, order, spectra)


def left_operand(real, imag):
    stacked = jnp.concatenate(
        [
            jnp.concatenate([real, imag], axis=1),
            jnp.concatenate([imag, -real], axis=1),
        ],
        axis=0,
    )
    return halves(stacked)


def right_operand(real, imag):
    return halves(jnp.concatenate([real, imag], axis=1))


def product(left, right):
    dims = ((1,), (1,))
    return (
        dot(left[0], right[0], dims)
        + dot(left[0], right[1], dims)
        + dot(left[1], right[0], dims)
    )


def packed_rows(scratch, lead, first, rows, group, count):
    pieces = [
        scratch[lead, pl.ds(first + group * 8 + step, count, stride=rows), :][:, :rows]
        for step in range(8)
    ]
    return jnp.concatenate(pieces, axis=1)


def self_kernel(place, *refs):
    chunks, (same, other), scratch = refs[:MEMBERS], refs[MEMBERS:-1], refs[-1]
    _, bins, rows, _ = chunks[0].shape
    half = rows // 2
    count = 2 * bins
    width = 8 * rows
    for distance in range(MEMBERS):
        chunk = chunks[distance]
        block = (MEMBERS - distance) % MEMBERS
        for slot in range(bins):
            real, imag = chunk[0, slot], chunk[1, slot]
            value = product(left_operand(real, imag), right_operand(real, imag))
            scratch[distance, slot * 2 * rows : (slot + 1) * 2 * rows, 0:rows] = value
        for out, shift in ((same, 0), (other, 1)):
            first = lax.rem(place[1] + shift, 2) * half
            for group in range(half // 8):
                out[block * count : (block + 1) * count, group * width : (group + 1) * width] = (
                    packed_rows(scratch, distance, first, rows, group, count)
                )


def pair_kernel(place, *refs):
    blocks, outs, scratch = refs[:MEMBERS], refs[MEMBERS:-1], refs[-1]
    _, bins, rows, _ = blocks[0].shape
    half = rows // 2
    count = 2 * bins
    width = 8 * rows
    for slot in range(bins):
        rights = []
        lefts = []
        for block in blocks:
            real, imag = block[0, slot], block[1, slot]
            rights.append(right_operand(real, imag))
            lefts.append(left_operand(real, imag))
        for owner in range(MEMBERS):
            for pair in range(2):
                partner = (owner + pair + 1) % MEMBERS
                scratch[owner * 2 + pair, slot * 2 * rows : (slot + 1) * 2 * rows, 0:rows] = (
                    product(lefts[owner], rights[partner])
                )
    for at, (owner, shift, pairs) in enumerate(PIECES):
        first = lax.rem(place[1] + shift, 2) * half
        for row, pair in enumerate(pairs):
            for group in range(half // 8):
                outs[at][row, :, group * width : (group + 1) * width] = (
                    packed_rows(scratch, owner * 2 + pair, first, rows, group, count)
                )


def extra_kernel(place, mine, theirs, same, other, scratch):
    _, bins, rows, _ = mine.shape
    half = rows // 2
    count = 2 * bins
    width = 8 * rows
    even = lax.rem(place[0], 2) == 0
    for slot in range(bins):
        first = [jnp.where(even, mine[part, slot], theirs[part, slot]) for part in range(2)]
        second = [jnp.where(even, theirs[part, slot], mine[part, slot]) for part in range(2)]
        value = product(left_operand(*first), right_operand(*second))
        scratch[0, slot * 2 * rows : (slot + 1) * 2 * rows, 0:rows] = value
    for out, shift in ((same, 0), (other, 1)):
        start = lax.rem(place[1] + shift, 2) * half
        for group in range(half // 8):
            out[0, :, group * width : (group + 1) * width] = (
                packed_rows(scratch, 0, start, rows, group, count)
            )


def self_pairs(place, chunks):
    _, bins, rows, windows = chunks[0].shape
    columns = rows * rows // 2
    shape = jax.ShapeDtypeStruct((MEMBERS * 2 * bins, columns), F32)
    flops = MEMBERS * bins * 3 * 2 * 4 * rows * rows * windows
    return pl.pallas_call(
        self_kernel,
        out_shape=(shape, shape),
        in_specs=[SMEM] + [VMEM] * MEMBERS,
        out_specs=(VMEM, VMEM),
        scratch_shapes=[pltpu.VMEM((MEMBERS, 2 * bins * rows, 128), F32)],
        compiler_params=pltpu.CompilerParams(vmem_limit_bytes=LIMIT),
        cost_estimate=pl.CostEstimate(flops=flops * 8, bytes_accessed=1 << 22, transcendentals=0),
        name="self_pairs",
    )(place, *chunks)


def partner_pairs(place, blocks):
    _, bins, rows, windows = blocks[0].shape
    columns = rows * rows // 2
    shapes = tuple(
        jax.ShapeDtypeStruct((len(pairs), 2 * bins, columns), F32) for _, _, pairs in PIECES
    )
    flops = 2 * MEMBERS * bins * 3 * 2 * 4 * rows * rows * windows
    return pl.pallas_call(
        pair_kernel,
        out_shape=shapes,
        in_specs=[SMEM] + [VMEM] * MEMBERS,
        out_specs=(VMEM,) * len(PIECES),
        scratch_shapes=[pltpu.VMEM((2 * MEMBERS, 2 * bins * rows, 128), F32)],
        compiler_params=pltpu.CompilerParams(vmem_limit_bytes=LIMIT),
        cost_estimate=pl.CostEstimate(flops=flops, bytes_accessed=1 << 22, transcendentals=0),
        name="partner_pairs",
    )(place, *blocks)


def extra_pairs(place, mine, theirs):
    _, bins, rows, windows = mine.shape
    shape = jax.ShapeDtypeStruct((1, 2 * bins, rows * rows // 2), F32)
    return pl.pallas_call(
        extra_kernel,
        out_shape=(shape, shape),
        in_specs=[SMEM, VMEM, VMEM],
        out_specs=(VMEM, VMEM),
        scratch_shapes=[pltpu.VMEM((1, 2 * bins * rows, 128), F32)],
        compiler_params=pltpu.CompilerParams(vmem_limit_bytes=LIMIT),
        name="extra_pairs",
    )(place, mine, theirs)


def lag_kernel(place, table, same, other, *refs):
    pieces, extras, out = refs[: len(PIECES)], refs[len(PIECES) : -1], refs[-1]
    columns = out.shape[2]
    tile = 640 if columns % 640 == 0 else columns
    high, low = halves(table[...])
    dims = ((1,), (0,))
    even = lax.rem(place[0], 2) == 0
    found = {}
    for piece, (distance, shift, pairs) in zip(pieces, PIECES):
        for row, pair in enumerate(pairs):
            found[pair, shift, distance] = piece, row
    own_same, own_other, theirs_same, theirs_other = extras
    more = {(1, 0): theirs_same, (1, 1): theirs_other, (2, 0): own_same, (2, 1): own_other}
    for pair in range(3):
        for at in range(0, columns, tile):
            span = slice(at, at + tile)
            if pair == 0:
                stacked = jnp.concatenate([same[:, span], other[:, span]], axis=0)
            else:
                terms = []
                for shift in range(2):
                    for distance in range(MEMBERS):
                        piece, row = found[pair - 1, shift, distance]
                        term = piece[row, :, span]
                        if pair == 1 and (distance, shift) in more:
                            term = jnp.where(even, more[distance, shift][0, :, span], term)
                        terms.append(term)
                stacked = jnp.concatenate(terms, axis=0)
            first, second = halves(stacked)
            out[pair, :, span] = dot(high, first, dims) + dot(high, second, dims) + dot(low, first, dims)


def lag_transform(place, table, same, other, pieces):
    lags = table.shape[0]
    columns = same.shape[1]
    return pl.pallas_call(
        lag_kernel,
        out_shape=jax.ShapeDtypeStruct((3, lags, columns), F32),
        in_specs=[SMEM] + [VMEM] * (3 + len(pieces)),
        out_specs=VMEM,
        compiler_params=pltpu.CompilerParams(vmem_limit_bytes=LIMIT),
        name="lag_transform",
    )(place, table, same, other, *pieces)


def lag_table(bin_assign, member, band, factor):
    bins = bin_assign.shape[0]
    lags = 2 * bins
    chunk = bins // (2 * MEMBERS)
    column = jnp.arange(lags, dtype=jnp.int32)
    shift = column // (MEMBERS * 2 * chunk)
    distance = column // (2 * chunk) % MEMBERS
    slot = column // 2 % chunk
    part = column % 2
    where = (band + shift) % 2 * (MEMBERS * chunk) + (member - distance + MEMBERS) % MEMBERS * chunk + slot
    steps = jnp.arange(lags, dtype=jnp.int32)
    phase = steps[:, None] * bin_assign[where][None, :] % lags
    angles = phase.astype(F32) * (2.0 * math.pi / lags)
    return jnp.where(part[None, :] == 0, jnp.cos(angles), -jnp.sin(angles)) * factor


def moved(array, loop_size, distance, shift, wanted):
    quarter = loop_size // MEMBERS
    route = [
        (i * 2 + j, (i + distance(i // quarter) * quarter) % loop_size * 2 + (j + shift) % 2)
        for i in range(loop_size)
        for j in range(2)
        if wanted(i // quarter)
    ]
    return lax.ppermute(array, ("chan", "band"), route)


def on_device(loop_size, spectra, channel_order, bin_assign):
    member = lax.axis_index("chan") // (loop_size // MEMBERS)
    band = lax.axis_index("band")
    even = member % 2 == 0
    every = lambda m: True
    away = [lax.rem(member + distance, MEMBERS) for distance in range(MEMBERS)]
    swapped = jnp.where(even, away[3], away[1])
    place = jnp.stack([member, band, *away, swapped]).astype(jnp.int32)
    blocks = [None] * MEMBERS
    chunks = [None] * MEMBERS
    for distance in (2, 3, 1):
        chunks[distance] = ordered_chunk(place, channel_order, spectra, distance)
        blocks[MEMBERS - distance] = moved(
            chunks[distance], loop_size, lambda m: distance, 0, every
        )
    swap = ordered_chunk(place, channel_order, spectra, MEMBERS)
    theirs = moved(swap, loop_size, lambda m: 1 if m % 2 == 0 else -1, 0, every)
    blocks[0] = chunks[0] = ordered_chunk(place, channel_order, spectra, 0)
    same, other = self_pairs(place, chunks)
    other = moved(other, loop_size, lambda m: 0, 1, every)
    own_same, own_other = extra_pairs(place, chunks[2], theirs)
    odd = lambda m: m % 2 == 1
    theirs_same = moved(own_same, loop_size, lambda m: -1, 0, odd)
    theirs_other = moved(own_other, loop_size, lambda m: -1, 1, odd)
    own_other = moved(own_other, loop_size, lambda m: 0, 1, every)
    results = partner_pairs(place, blocks)
    pieces = []
    for piece, (distance, shift, pairs) in zip(results, PIECES):
        wanted = every
        if pairs == (0,):
            wanted = lambda m: (m + distance) % 2 == 1
        if distance or shift:
            piece = moved(piece, loop_size, lambda m: distance, shift, wanted)
        pieces.append(piece)
    pieces += [own_same, own_other, theirs_same, theirs_other]
    table = lag_table(bin_assign, member, band, 1.0 / spectra.shape[3])
    return lag_transform(place, table, same, other, pieces)[None]


def solution(mesh):
    in_specs = (P(None, "band", ("grp", "chan"), None), P(("grp", "chan"), None), P())
    out_specs = P(("grp", "chan"), None, None, "band")
    return jax.shard_map(
        functools.partial(on_device, mesh.shape["chan"]),
        mesh=mesh,
        in_specs=in_specs,
        out_specs=out_specs,
        check_vma=False,
    )
```

```python
import functools
import math

import jax
import jax.numpy as jnp
from jax import lax
from jax.experimental import pallas as pl
from jax.experimental.pallas import tpu as pltpu
from jax.sharding import PartitionSpec as P

MEMBERS = 4
F32 = jnp.float32
BF16 = jnp.bfloat16
VMEM = pl.BlockSpec(memory_space=pltpu.VMEM)
SMEM = pl.BlockSpec(memory_space=pltpu.SMEM)
PIECES = [
    (2, 0, (1,)),
    (2, 1, (1,)),
    (2, 0, (0,)),
    (2, 1, (0,)),
    (1, 0, (1,)),
    (1, 1, (1,)),
    (3, 0, (0, 1)),
    (3, 1, (0, 1)),
    (1, 0, (0,)),
    (1, 1, (0,)),
    (0, 1, (0, 1)),
    (0, 0, (0, 1)),
]
LIMIT = 40 * 1024 * 1024


def halves(x):
    high = x.astype(BF16)
    low = (x - high.astype(F32)).astype(BF16)
    return high, low


def thirds(x):
    high = x.astype(BF16)
    rest = x - high.astype(F32)
    middle = rest.astype(BF16)
    low = (rest - middle.astype(F32)).astype(BF16)
    return high, middle, low


def dot(left, right, dims):
    return lax.dot_general(left, right, (dims, ((), ())), preferred_element_type=F32)


def order_kernel(which, place, order, spectra, ordered):
    parts, bins, rows, _ = ordered.shape
    chunk = place[2 + which]
    row_ids = lax.broadcasted_iota(jnp.int32, (rows, rows), 0)
    chosen = jnp.where(row_ids == order[...], 1.0, 0.0).astype(BF16)
    chosen = jnp.concatenate([chosen] * 3, axis=0)
    for part in range(parts):
        for slot in range(bins):
            values = spectra[part, chunk * bins + slot]
            stacked = jnp.concatenate(thirds(values), axis=0)
            ordered[part, slot] = dot(chosen, stacked, ((0,), (0,)))


def ordered_chunk(place, order, spectra, which):
    parts, bins, rows, windows = spectra.shape
    return pl.pallas_call(
        functools.partial(order_kernel, which),
        out_shape=jax.ShapeDtypeStruct((parts, bins // MEMBERS, rows, windows), F32),
        in_specs=[SMEM, VMEM, VMEM],
        out_specs=VMEM,
        compiler_params=pltpu.CompilerParams(vmem_limit_bytes=LIMIT),
        name=f"order_{which}",
    )(place, order, spectra)


def left_operand(real, imag):
    stacked = jnp.concatenate(
        [
            jnp.concatenate([real, imag], axis=1),
            jnp.concatenate([imag, -real], axis=1),
        ],
        axis=0,
    )
    return halves(stacked)


def right_operand(real, imag):
    return halves(jnp.concatenate([real, imag], axis=1))


def product(left, right):
    dims = ((1,), (1,))
    return (
        dot(left[0], right[0], dims)
        + dot(left[0], right[1], dims)
        + dot(left[1], right[0], dims)
    )


def packed_rows(scratch, lead, first, rows, group, count):
    pieces = [
        scratch[lead, pl.ds(first + group * 8 + step, count, stride=rows), :][:, :rows]
        for step in range(8)
    ]
    return jnp.concatenate(pieces, axis=1)


def self_kernel(place, *refs):
    chunks, (same, other), scratch = refs[:MEMBERS], refs[MEMBERS:-1], refs[-1]
    _, bins, rows, _ = chunks[0].shape
    half = rows // 2
    count = 2 * bins
    width = 8 * rows
    for distance in range(MEMBERS):
        chunk = chunks[distance]
        block = (MEMBERS - distance) % MEMBERS
        for slot in range(bins):
            real, imag = chunk[0, slot], chunk[1, slot]
            value = product(left_operand(real, imag), right_operand(real, imag))
            scratch[distance, slot * 2 * rows : (slot + 1) * 2 * rows, 0:rows] = value
        for out, shift in ((same, 0), (other, 1)):
            first = lax.rem(place[1] + shift, 2) * half
            for group in range(half // 8):
                out[block * count : (block + 1) * count, group * width : (group + 1) * width] = (
                    packed_rows(scratch, distance, first, rows, group, count)
                )


def pair_kernel(place, *refs):
    blocks, outs, scratch = refs[:MEMBERS], refs[MEMBERS:-1], refs[-1]
    _, bins, rows, _ = blocks[0].shape
    half = rows // 2
    count = 2 * bins
    width = 8 * rows
    for slot in range(bins):
        rights = []
        lefts = []
        for block in blocks:
            real, imag = block[0, slot], block[1, slot]
            rights.append(right_operand(real, imag))
            lefts.append(left_operand(real, imag))
        for owner in range(MEMBERS):
            for pair in range(2):
                partner = (owner + pair + 1) % MEMBERS
                scratch[owner * 2 + pair, slot * 2 * rows : (slot + 1) * 2 * rows, 0:rows] = (
                    product(lefts[owner], rights[partner])
                )
    for at, (owner, shift, pairs) in enumerate(PIECES):
        first = lax.rem(place[1] + shift, 2) * half
        for row, pair in enumerate(pairs):
            for group in range(half // 8):
                outs[at][row, :, group * width : (group + 1) * width] = (
                    packed_rows(scratch, owner * 2 + pair, first, rows, group, count)
                )


def extra_kernel(place, mine, theirs, same, other, scratch):
    _, bins, rows, _ = mine.shape
    half = rows // 2
    count = 2 * bins
    width = 8 * rows
    even = lax.rem(place[0], 2) == 0
    for slot in range(bins):
        first = [jnp.where(even, mine[part, slot], theirs[part, slot]) for part in range(2)]
        second = [jnp.where(even, theirs[part, slot], mine[part, slot]) for part in range(2)]
        value = product(left_operand(*first), right_operand(*second))
        scratch[0, slot * 2 * rows : (slot + 1) * 2 * rows, 0:rows] = value
    for out, shift in ((same, 0), (other, 1)):
        start = lax.rem(place[1] + shift, 2) * half
        for group in range(half // 8):
            out[0, :, group * width : (group + 1) * width] = (
                packed_rows(scratch, 0, start, rows, group, count)
            )


def self_pairs(place, chunks):
    _, bins, rows, windows = chunks[0].shape
    columns = rows * rows // 2
    shape = jax.ShapeDtypeStruct((MEMBERS * 2 * bins, columns), F32)
    flops = MEMBERS * bins * 3 * 2 * 4 * rows * rows * windows
    return pl.pallas_call(
        self_kernel,
        out_shape=(shape, shape),
        in_specs=[SMEM] + [VMEM] * MEMBERS,
        out_specs=(VMEM, VMEM),
        scratch_shapes=[pltpu.VMEM((MEMBERS, 2 * bins * rows, 128), F32)],
        compiler_params=pltpu.CompilerParams(vmem_limit_bytes=LIMIT),
        cost_estimate=pl.CostEstimate(flops=flops * 8, bytes_accessed=1 << 22, transcendentals=0),
        name="self_pairs",
    )(place, *chunks)


def partner_pairs(place, blocks):
    _, bins, rows, windows = blocks[0].shape
    columns = rows * rows // 2
    shapes = tuple(
        jax.ShapeDtypeStruct((len(pairs), 2 * bins, columns), F32) for _, _, pairs in PIECES
    )
    flops = 2 * MEMBERS * bins * 3 * 2 * 4 * rows * rows * windows
    return pl.pallas_call(
        pair_kernel,
        out_shape=shapes,
        in_specs=[SMEM] + [VMEM] * MEMBERS,
        out_specs=(VMEM,) * len(PIECES),
        scratch_shapes=[pltpu.VMEM((2 * MEMBERS, 2 * bins * rows, 128), F32)],
        compiler_params=pltpu.CompilerParams(vmem_limit_bytes=LIMIT),
        cost_estimate=pl.CostEstimate(flops=flops, bytes_accessed=1 << 22, transcendentals=0),
        name="partner_pairs",
    )(place, *blocks)


def extra_pairs(place, mine, theirs):
    _, bins, rows, windows = mine.shape
    shape = jax.ShapeDtypeStruct((1, 2 * bins, rows * rows // 2), F32)
    return pl.pallas_call(
        extra_kernel,
        out_shape=(shape, shape),
        in_specs=[SMEM, VMEM, VMEM],
        out_specs=(VMEM, VMEM),
        scratch_shapes=[pltpu.VMEM((1, 2 * bins * rows, 128), F32)],
        compiler_params=pltpu.CompilerParams(vmem_limit_bytes=LIMIT),
        name="extra_pairs",
    )(place, mine, theirs)


def lag_kernel(place, table, same, other, *refs):
    pieces, extras, out = refs[: len(PIECES)], refs[len(PIECES) : -1], refs[-1]
    columns = out.shape[2]
    tile = 640 if columns % 640 == 0 else columns
    high, low = halves(table[...])
    dims = ((1,), (0,))
    even = lax.rem(place[0], 2) == 0
    found = {}
    for piece, (distance, shift, pairs) in zip(pieces, PIECES):
        for row, pair in enumerate(pairs):
            found[pair, shift, distance] = piece, row
    own_same, own_other, theirs_same, theirs_other = extras
    more = {(1, 0): theirs_same, (1, 1): theirs_other, (2, 0): own_same, (2, 1): own_other}
    for pair in range(3):
        for at in range(0, columns, tile):
            span = slice(at, at + tile)
            if pair == 0:
                stacked = jnp.concatenate([same[:, span], other[:, span]], axis=0)
            else:
                terms = []
                for shift in range(2):
                    for distance in range(MEMBERS):
                        piece, row = found[pair - 1, shift, distance]
                        term = piece[row, :, span]
                        if pair == 1 and (distance, shift) in more:
                            term = jnp.where(even, more[distance, shift][0, :, span], term)
                        terms.append(term)
                stacked = jnp.concatenate(terms, axis=0)
            first, second = halves(stacked)
            out[pair, :, span] = dot(high, first, dims) + dot(high, second, dims) + dot(low, first, dims)


def lag_transform(place, table, same, other, pieces):
    lags = table.shape[0]
    columns = same.shape[1]
    return pl.pallas_call(
        lag_kernel,
        out_shape=jax.ShapeDtypeStruct((3, lags, columns), F32),
        in_specs=[SMEM] + [VMEM] * (3 + len(pieces)),
        out_specs=VMEM,
        compiler_params=pltpu.CompilerParams(vmem_limit_bytes=LIMIT),
        name="lag_transform",
    )(place, table, same, other, *pieces)


def lag_table(bin_assign, member, band, factor):
    bins = bin_assign.shape[0]
    lags = 2 * bins
    chunk = bins // (2 * MEMBERS)
    column = jnp.arange(lags, dtype=jnp.int32)
    shift = column // (MEMBERS * 2 * chunk)
    distance = column // (2 * chunk) % MEMBERS
    slot = column // 2 % chunk
    part = column % 2
    where = (band + shift) % 2 * (MEMBERS * chunk) + (member - distance + MEMBERS) % MEMBERS * chunk + slot
    steps = jnp.arange(lags, dtype=jnp.int32)
    phase = steps[:, None] * bin_assign[where][None, :] % lags
    angles = phase.astype(F32) * (2.0 * math.pi / lags)
    return jnp.where(part[None, :] == 0, jnp.cos(angles), -jnp.sin(angles)) * factor


def deliver_kernel(loop_size, moves, *refs):
    count = len(moves)
    sources, targets = refs[:count], refs[count : 2 * count]
    send_sems, recv_sems = refs[2 * count :]
    quarter = loop_size // MEMBERS
    chan = lax.axis_index("chan")
    band = lax.axis_index("band")
    odd = lax.rem(chan // quarter, 2)

    def device(distance, shift):
        where = lax.rem(chan + distance * quarter, loop_size)
        return {"chan": where, "band": lax.rem(band + shift, 2)}

    barrier = pltpu.get_barrier_semaphore()
    for distance in range(MEMBERS):
        for shift in range(2):
            if distance or shift:
                pl.semaphore_signal(
                    barrier,
                    inc=1,
                    device_id=device(distance, shift),
                    device_id_type=pl.DeviceIdType.MESH,
                )
    pl.semaphore_wait(barrier, 2 * MEMBERS - 1)

    def guarded(parity, action):
        if parity is None:
            action()
        else:
            pl.when(odd == parity)(action)

    copies = []
    for at, (distance, shift, parity) in enumerate(moves):
        copy = pltpu.make_async_remote_copy(
            src_ref=sources[at],
            dst_ref=targets[at],
            send_sem=send_sems.at[at],
            recv_sem=recv_sems.at[at],
            device_id=device(distance, shift),
            device_id_type=pl.DeviceIdType.MESH,
        )
        copies.append(copy)
        guarded(parity, copy.start)
    for copy, (distance, shift, parity) in zip(copies, moves):
        guarded(parity, copy.wait_send)
        guarded(None if parity is None else (parity + distance) % 2, copy.wait_recv)


def deliver(loop_size, moves, arrays):
    count = len(moves)
    return pl.pallas_call(
        functools.partial(deliver_kernel, loop_size, moves),
        out_shape=tuple(jax.ShapeDtypeStruct(array.shape, array.dtype) for array in arrays),
        in_specs=[VMEM] * count,
        out_specs=(VMEM,) * count,
        scratch_shapes=[pltpu.SemaphoreType.DMA((count,)), pltpu.SemaphoreType.DMA((count,))],
        compiler_params=pltpu.CompilerParams(
            collective_id=0, has_side_effects=True, vmem_limit_bytes=LIMIT
        ),
        name="deliver",
    )(*arrays)


def moved(array, loop_size, distance, shift, wanted):
    quarter = loop_size // MEMBERS
    route = [
        (i * 2 + j, (i + distance(i // quarter) * quarter) % loop_size * 2 + (j + shift) % 2)
        for i in range(loop_size)
        for j in range(2)
        if wanted(i // quarter)
    ]
    return lax.ppermute(array, ("chan", "band"), route)


def on_device(loop_size, spectra, channel_order, bin_assign):
    member = lax.axis_index("chan") // (loop_size // MEMBERS)
    band = lax.axis_index("band")
    even = member % 2 == 0
    every = lambda m: True
    away = [lax.rem(member + distance, MEMBERS) for distance in range(MEMBERS)]
    swapped = jnp.where(even, away[3], away[1])
    place = jnp.stack([member, band, *away, swapped]).astype(jnp.int32)
    blocks = [None] * MEMBERS
    chunks = [None] * MEMBERS
    for distance in (2, 3, 1):
        chunks[distance] = ordered_chunk(place, channel_order, spectra, distance)
        blocks[MEMBERS - distance] = moved(
            chunks[distance], loop_size, lambda m: distance, 0, every
        )
    swap = ordered_chunk(place, channel_order, spectra, MEMBERS)
    theirs = moved(swap, loop_size, lambda m: 1 if m % 2 == 0 else -1, 0, every)
    blocks[0] = chunks[0] = ordered_chunk(place, channel_order, spectra, 0)
    same, other = self_pairs(place, chunks)
    own_same, own_other = extra_pairs(place, chunks[2], theirs)
    results = partner_pairs(place, blocks)
    moves, arrays = [], []
    for piece, (distance, shift, pairs) in zip(results, PIECES):
        if distance or shift:
            moves.append((distance, shift, (distance + 1) % 2 if pairs == (0,) else None))
            arrays.append(piece)
    moves += [(3, 0, 1), (3, 1, 1), (0, 1, 0), (0, 1, None)]
    arrays += [own_same, own_other, own_other, other]
    *pieces, theirs_same, theirs_other, own_other, other = deliver(loop_size, moves, arrays)
    pieces += [results[-1], own_same, own_other, theirs_same, theirs_other]
    table = lag_table(bin_assign, member, band, 1.0 / spectra.shape[3])
    return lag_transform(place, table, same, other, pieces)[None]


def solution(mesh):
    in_specs = (P(None, "band", ("grp", "chan"), None), P(("grp", "chan"), None), P())
    out_specs = P(("grp", "chan"), None, None, "band")
    return jax.shard_map(
        functools.partial(on_device, mesh.shape["chan"]),
        mesh=mesh,
        in_specs=in_specs,
        out_specs=out_specs,
        check_vma=False,
    )
```

```python
import functools
import math

import jax
import jax.numpy as jnp
from jax import lax
from jax.experimental import pallas as pl
from jax.experimental.pallas import tpu as pltpu
from jax.sharding import PartitionSpec as P

MEMBERS = 4
F32 = jnp.float32
BF16 = jnp.bfloat16
VMEM = pl.BlockSpec(memory_space=pltpu.VMEM)
SMEM = pl.BlockSpec(memory_space=pltpu.SMEM)
PIECES = [
    (2, 0, (1,)),
    (2, 1, (1,)),
    (2, 0, (0,)),
    (2, 1, (0,)),
    (1, 0, (1,)),
    (1, 1, (1,)),
    (3, 0, (0, 1)),
    (3, 1, (0, 1)),
    (1, 0, (0,)),
    (1, 1, (0,)),
    (0, 1, (0, 1)),
    (0, 0, (0, 1)),
]
LIMIT = 40 * 1024 * 1024


def halves(x):
    high = x.astype(BF16)
    low = (x - high.astype(F32)).astype(BF16)
    return high, low


def thirds(x):
    high = x.astype(BF16)
    rest = x - high.astype(F32)
    middle = rest.astype(BF16)
    low = (rest - middle.astype(F32)).astype(BF16)
    return high, middle, low


def dot(left, right, dims):
    return lax.dot_general(left, right, (dims, ((), ())), preferred_element_type=F32)


def ordered_rows(chosen, values):
    stacked = jnp.concatenate(thirds(values), axis=0)
    return dot(chosen, stacked, ((0,), (0,)))


def left_operand(real, imag):
    stacked = jnp.concatenate(
        [
            jnp.concatenate([real, imag], axis=1),
            jnp.concatenate([imag, -real], axis=1),
        ],
        axis=0,
    )
    return halves(stacked)


def right_operand(real, imag):
    return halves(jnp.concatenate([real, imag], axis=1))


def product(left, right):
    dims = ((1,), (1,))
    return (
        dot(left[0], right[0], dims)
        + dot(left[0], right[1], dims)
        + dot(left[1], right[0], dims)
    )


def packed_rows(scratch, lead, first, rows, group, count):
    pieces = [
        scratch[lead, pl.ds(first + group * 8 + step, count, stride=rows), :][:, :rows]
        for step in range(8)
    ]
    return jnp.concatenate(pieces, axis=1)


def put_product(scratch, lead, slot, value):
    rows = value.shape[1]
    scratch[lead, slot * 2 * rows : (slot + 1) * 2 * rows, 0:rows] = value


def exchange_kernel(loop_size, moves, order, spectra, *refs):
    count = len(moves)
    same, own_same, kept = refs[:3]
    targets = refs[3 : 3 + count]
    sources = refs[3 + count : 3 + 2 * count]
    chunks, blocks, scratch, send_sems, recv_sems, go_sems, come_sems = refs[3 + 2 * count :]
    _, bins, _, rows, _ = chunks.shape
    half = rows // 2
    packed = 2 * bins
    width = 8 * rows
    quarter = loop_size // MEMBERS
    chan = lax.axis_index("chan")
    band = lax.axis_index("band")
    member = chan // quarter
    parity = lax.rem(member, 2)
    even = parity == 0
    swap = 1 - 2 * parity

    def device(distance, shift):
        where = lax.rem(chan + distance * quarter + loop_size, loop_size)
        return {"chan": where, "band": lax.rem(band + shift, 2)}

    def send(source, target, send_sem, recv_sem, where):
        return pltpu.make_async_remote_copy(
            src_ref=source,
            dst_ref=target,
            send_sem=send_sem,
            recv_sem=recv_sem,
            device_id=where,
            device_id_type=pl.DeviceIdType.MESH,
        )

    barrier = pltpu.get_barrier_semaphore()
    for distance in range(MEMBERS):
        for shift in range(2):
            if distance or shift:
                pl.semaphore_signal(
                    barrier,
                    inc=1,
                    device_id=device(distance, shift),
                    device_id_type=pl.DeviceIdType.MESH,
                )

    row_ids = lax.broadcasted_iota(jnp.int32, (rows, rows), 0)
    chosen = jnp.where(row_ids == order[...], 1.0, 0.0).astype(BF16)
    chosen = jnp.concatenate([chosen] * 3, axis=0)

    def arrange(which, slot):
        if which == MEMBERS:
            chunk = lax.rem(member + 3 - 2 * parity, MEMBERS)
        else:
            chunk = lax.rem(member + which, MEMBERS)
        for part in range(2):
            values = spectra[part, chunk * bins + slot]
            chunks[which, slot, part] = ordered_rows(chosen, values)

    forward = {}
    for slot in range(bins):
        for which in (2, 3, 1, MEMBERS):
            arrange(which, slot)
            landing = 0 if which == MEMBERS else MEMBERS - which
            at = slot * MEMBERS + landing
            forward[slot, landing] = send(
                chunks.at[which, slot],
                blocks.at[landing, slot],
                go_sems.at[at],
                come_sems.at[at],
                device(swap if which == MEMBERS else which, 0),
            )
        if slot == 0:
            pl.semaphore_wait(barrier, 2 * MEMBERS - 1)
        for landing in (2, 1, 3, 0):
            forward[slot, landing].start()

    def guarded(wanted, action):
        if wanted is None:
            action()
        else:
            pl.when(parity == wanted)(action)

    def start(at):
        distance, shift, wanted = moves[at]
        copy = send(
            sources[at], targets[at], send_sems.at[at], recv_sems.at[at], device(distance, shift)
        )
        guarded(wanted, copy.start)
        return copy

    def fill(out, row, lead, shift):
        first = lax.rem(band + shift, 2) * half
        for group in range(half // 8):
            out[row, :, group * width : (group + 1) * width] = (
                packed_rows(scratch, lead, first, rows, group, packed)
            )

    returns = [None] * count
    for distance in range(MEMBERS):
        for slot in range(bins):
            if distance == 0:
                arrange(0, slot)
            real, imag = chunks[distance, slot, 0], chunks[distance, slot, 1]
            put_product(
                scratch,
                2 * MEMBERS + 1 + distance,
                slot,
                product(left_operand(real, imag), right_operand(real, imag)),
            )
        block = (MEMBERS - distance) % MEMBERS
        fill(same, block, 2 * MEMBERS + 1 + distance, 0)
        fill(sources[count - 1], block, 2 * MEMBERS + 1 + distance, 1)
    returns[count - 1] = start(count - 1)

    for slot in range(bins):
        for landing in (2, 1, 3, 0):
            forward[slot, landing].wait_recv()
        lefts, rights = [], []
        for at in range(MEMBERS):
            block = blocks if at else chunks
            real, imag = block[at, slot, 0], block[at, slot, 1]
            lefts.append(left_operand(real, imag))
            rights.append(right_operand(real, imag))
        for owner in (2, 1, 3, 0):
            for pair in range(2):
                partner = (owner + pair + 1) % MEMBERS
                put_product(scratch, owner * 2 + pair, slot, product(lefts[owner], rights[partner]))
        mine = [chunks[2, slot, part] for part in range(2)]
        theirs = [blocks[0, slot, part] for part in range(2)]
        first = [jnp.where(even, a, b) for a, b in zip(mine, theirs)]
        second = [jnp.where(even, b, a) for a, b in zip(mine, theirs)]
        put_product(
            scratch, 2 * MEMBERS, slot, product(left_operand(*first), right_operand(*second))
        )

    for at, (owner, shift, pairs) in enumerate(PIECES[:-1]):
        for row, pair in enumerate(pairs):
            fill(sources[at], row, owner * 2 + pair, shift)
        returns[at] = start(at)
    fill(own_same, 0, 2 * MEMBERS, 0)
    base = len(PIECES) - 1
    fill(sources[base], 0, 2 * MEMBERS, 0)
    returns[base] = start(base)
    fill(sources[base + 1], 0, 2 * MEMBERS, 1)
    fill(sources[base + 2], 0, 2 * MEMBERS, 1)
    returns[base + 1] = start(base + 1)
    returns[base + 2] = start(base + 2)
    for row, pair in enumerate(PIECES[-1][2]):
        fill(kept, row, pair, 0)

    for copy in forward.values():
        copy.wait_send()
    for copy, (distance, shift, wanted) in zip(returns, moves):
        guarded(wanted, copy.wait_send)
        guarded(None if wanted is None else (wanted + distance) % 2, copy.wait_recv)


def exchange(loop_size, order, spectra):
    _, bins, rows, windows = spectra.shape
    bins = bins // MEMBERS
    columns = rows * rows // 2
    moves, leads = [], []
    for distance, shift, pairs in PIECES[:-1]:
        moves.append((distance, shift, (distance + 1) % 2 if pairs == (0,) else None))
        leads.append(len(pairs))
    moves += [(3, 0, 1), (3, 1, 1), (0, 1, 0), (0, 1, None)]
    leads += [1, 1, 1, MEMBERS]
    count = len(moves)
    outs = [(lead, 2 * bins, columns) for lead in [MEMBERS, 1, 2] + leads]
    results = pl.pallas_call(
        functools.partial(exchange_kernel, loop_size, moves),
        out_shape=tuple(jax.ShapeDtypeStruct(shape, F32) for shape in outs),
        in_specs=[VMEM, VMEM],
        out_specs=(VMEM,) * len(outs),
        scratch_shapes=[pltpu.VMEM((lead, 2 * bins, columns), F32) for lead in leads]
        + [
            pltpu.VMEM((MEMBERS + 1, bins, 2, rows, windows), F32),
            pltpu.VMEM((MEMBERS, bins, 2, rows, windows), F32),
            pltpu.VMEM((3 * MEMBERS + 1, 2 * bins * rows, 128), F32),
            pltpu.SemaphoreType.DMA((count,)),
            pltpu.SemaphoreType.DMA((count,)),
            pltpu.SemaphoreType.DMA((bins * MEMBERS,)),
            pltpu.SemaphoreType.DMA((bins * MEMBERS,)),
        ],
        compiler_params=pltpu.CompilerParams(
            collective_id=0, has_side_effects=True, vmem_limit_bytes=LIMIT
        ),
        name="exchange",
    )(order, spectra)
    return results[:3], results[3:]


def lag_kernel(place, table, same, other, *refs):
    pieces, extras, out = refs[: len(PIECES)], refs[len(PIECES) : -1], refs[-1]
    columns = out.shape[2]
    tile = 640 if columns % 640 == 0 else columns
    high, low = halves(table[...])
    dims = ((1,), (0,))
    even = lax.rem(place[0], 2) == 0
    found = {}
    for piece, (distance, shift, pairs) in zip(pieces, PIECES):
        for row, pair in enumerate(pairs):
            found[pair, shift, distance] = piece, row
    own_same, own_other, theirs_same, theirs_other = extras
    more = {(1, 0): theirs_same, (1, 1): theirs_other, (2, 0): own_same, (2, 1): own_other}
    for pair in range(3):
        for at in range(0, columns, tile):
            span = slice(at, at + tile)
            if pair == 0:
                stacked = jnp.concatenate([same[:, span], other[:, span]], axis=0)
            else:
                terms = []
                for shift in range(2):
                    for distance in range(MEMBERS):
                        piece, row = found[pair - 1, shift, distance]
                        term = piece[row, :, span]
                        if pair == 1 and (distance, shift) in more:
                            term = jnp.where(even, more[distance, shift][0, :, span], term)
                        terms.append(term)
                stacked = jnp.concatenate(terms, axis=0)
            first, second = halves(stacked)
            out[pair, :, span] = dot(high, first, dims) + dot(high, second, dims) + dot(low, first, dims)


def lag_transform(place, table, same, other, pieces):
    lags = table.shape[0]
    columns = same.shape[1]
    return pl.pallas_call(
        lag_kernel,
        out_shape=jax.ShapeDtypeStruct((3, lags, columns), F32),
        in_specs=[SMEM] + [VMEM] * (3 + len(pieces)),
        out_specs=VMEM,
        compiler_params=pltpu.CompilerParams(vmem_limit_bytes=LIMIT),
        name="lag_transform",
    )(place, table, same, other, *pieces)


def lag_table(bin_assign, member, band, factor):
    bins = bin_assign.shape[0]
    lags = 2 * bins
    chunk = bins // (2 * MEMBERS)
    column = jnp.arange(lags, dtype=jnp.int32)
    shift = column // (MEMBERS * 2 * chunk)
    distance = column // (2 * chunk) % MEMBERS
    slot = column // 2 % chunk
    part = column % 2
    where = (band + shift) % 2 * (MEMBERS * chunk) + (member - distance + MEMBERS) % MEMBERS * chunk + slot
    steps = jnp.arange(lags, dtype=jnp.int32)
    phase = steps[:, None] * bin_assign[where][None, :] % lags
    angles = phase.astype(F32) * (2.0 * math.pi / lags)
    return jnp.where(part[None, :] == 0, jnp.cos(angles), -jnp.sin(angles)) * factor


def deliver_kernel(loop_size, moves, *refs):
    count = len(moves)
    sources, targets = refs[:count], refs[count : 2 * count]
    send_sems, recv_sems = refs[2 * count :]
    quarter = loop_size // MEMBERS
    chan = lax.axis_index("chan")
    band = lax.axis_index("band")
    odd = lax.rem(chan // quarter, 2)

    def device(distance, shift):
        where = lax.rem(chan + distance * quarter, loop_size)
        return {"chan": where, "band": lax.rem(band + shift, 2)}

    barrier = pltpu.get_barrier_semaphore()
    for distance in range(MEMBERS):
        for shift in range(2):
            if distance or shift:
                pl.semaphore_signal(
                    barrier,
                    inc=1,
                    device_id=device(distance, shift),
                    device_id_type=pl.DeviceIdType.MESH,
                )
    pl.semaphore_wait(barrier, 2 * MEMBERS - 1)

    def guarded(parity, action):
        if parity is None:
            action()
        else:
            pl.when(odd == parity)(action)

    copies = []
    for at, (distance, shift, parity) in enumerate(moves):
        copy = pltpu.make_async_remote_copy(
            src_ref=sources[at],
            dst_ref=targets[at],
            send_sem=send_sems.at[at],
            recv_sem=recv_sems.at[at],
            device_id=device(distance, shift),
            device_id_type=pl.DeviceIdType.MESH,
        )
        copies.append(copy)
        guarded(parity, copy.start)
    for copy, (distance, shift, parity) in zip(copies, moves):
        guarded(parity, copy.wait_send)
        guarded(None if parity is None else (parity + distance) % 2, copy.wait_recv)


def deliver(loop_size, moves, arrays):
    count = len(moves)
    return pl.pallas_call(
        functools.partial(deliver_kernel, loop_size, moves),
        out_shape=tuple(jax.ShapeDtypeStruct(array.shape, array.dtype) for array in arrays),
        in_specs=[VMEM] * count,
        out_specs=(VMEM,) * count,
        scratch_shapes=[pltpu.SemaphoreType.DMA((count,)), pltpu.SemaphoreType.DMA((count,))],
        compiler_params=pltpu.CompilerParams(
            collective_id=0, has_side_effects=True, vmem_limit_bytes=LIMIT
        ),
        name="deliver",
    )(*arrays)


def on_device(loop_size, spectra, channel_order, bin_assign):
    member = lax.axis_index("chan") // (loop_size // MEMBERS)
    band = lax.axis_index("band")
    place = jnp.stack([member, band]).astype(jnp.int32)
    local, returned = exchange(loop_size, channel_order, spectra)
    same, own_same, kept = local
    *pieces, theirs_same, theirs_other, own_other, other = returned
    pieces += [kept, own_same, own_other, theirs_same, theirs_other]
    table = lag_table(bin_assign, member, band, 1.0 / spectra.shape[3])
    flat = (MEMBERS * same.shape[1], same.shape[2])
    return lag_transform(place, table, same.reshape(flat), other.reshape(flat), pieces)[None]


def solution(mesh):
    in_specs = (P(None, "band", ("grp", "chan"), None), P(("grp", "chan"), None), P())
    out_specs = P(("grp", "chan"), None, None, "band")
    return jax.shard_map(
        functools.partial(on_device, mesh.shape["chan"]),
        mesh=mesh,
        in_specs=in_specs,
        out_specs=out_specs,
        check_vma=False,
    )
```

```python
import functools
import math

import jax
import jax.numpy as jnp
from jax import lax
from jax.experimental import pallas as pl
from jax.experimental.pallas import tpu as pltpu
from jax.sharding import PartitionSpec as P

MEMBERS = 4
F32 = jnp.float32
BF16 = jnp.bfloat16
VMEM = pl.BlockSpec(memory_space=pltpu.VMEM)
HBM = pl.BlockSpec(memory_space=pltpu.HBM)
SMEM = pl.BlockSpec(memory_space=pltpu.SMEM)
PIECES = [
    (2, 0, (1,)),
    (2, 1, (1,)),
    (2, 0, (0,)),
    (2, 1, (0,)),
    (1, 0, (1,)),
    (1, 1, (1,)),
    (3, 0, (0, 1)),
    (3, 1, (0, 1)),
    (1, 0, (0,)),
    (1, 1, (0,)),
    (0, 1, (0, 1)),
    (0, 0, (0, 1)),
]
LIMIT = 40 * 1024 * 1024


def halves(x):
    high = x.astype(BF16)
    low = (x - high.astype(F32)).astype(BF16)
    return high, low


def thirds(x):
    high = x.astype(BF16)
    rest = x - high.astype(F32)
    middle = rest.astype(BF16)
    low = (rest - middle.astype(F32)).astype(BF16)
    return high, middle, low


def dot(left, right, dims):
    return lax.dot_general(left, right, (dims, ((), ())), preferred_element_type=F32)


def ordered_rows(chosen, values):
    stacked = jnp.concatenate(thirds(values), axis=0)
    return dot(chosen, stacked, ((0,), (0,)))


def left_operand(real, imag):
    stacked = jnp.concatenate(
        [
            jnp.concatenate([real, imag], axis=1),
            jnp.concatenate([imag, -real], axis=1),
        ],
        axis=0,
    )
    return halves(stacked)


def right_operand(real, imag):
    return halves(jnp.concatenate([real, imag], axis=1))


def product(left, right):
    dims = ((1,), (1,))
    return (
        dot(left[0], right[0], dims)
        + dot(left[0], right[1], dims)
        + dot(left[1], right[0], dims)
    )


def packed_rows(scratch, lead, first, rows, group, count):
    pieces = [
        scratch[lead, pl.ds(first + group * 8 + step, count, stride=rows), :][:, :rows]
        for step in range(8)
    ]
    return jnp.concatenate(pieces, axis=1)


def put_product(scratch, lead, slot, value):
    rows = value.shape[1]
    scratch[lead, slot * 2 * rows : (slot + 1) * 2 * rows, 0:rows] = value


def lag_table(assign, member, band, bins, factor):
    total = assign.shape[1]
    lags = 2 * total
    column = lax.broadcasted_iota(jnp.int32, (total, lags), 1)
    shift = lax.div(column, MEMBERS * 2 * bins)
    distance = lax.rem(lax.div(column, 2 * bins), MEMBERS)
    slot = lax.rem(lax.div(column, 2), bins)
    chunk = lax.rem(member - distance + MEMBERS, MEMBERS)
    where = lax.rem(band + shift, 2) * (MEMBERS * bins) + chunk * bins + slot
    chosen = lax.broadcasted_iota(jnp.int32, (total, lags), 0) == where
    chosen = jnp.where(chosen, 1.0, 0.0).astype(BF16)
    many = jnp.broadcast_to(assign, (16, total)).astype(F32).astype(BF16)
    held = dot(many, chosen, ((1,), (0,)))[0:1, :]
    steps = lax.broadcasted_iota(jnp.int32, (lags, lags), 0).astype(F32)
    phase = steps * held
    phase = phase - jnp.floor(phase * (1.0 / lags)) * lags
    angles = phase * (2.0 * math.pi / lags)
    part = lax.rem(lax.broadcasted_iota(jnp.int32, (lags, lags), 1), 2)
    return jnp.where(part == 0, jnp.cos(angles), -jnp.sin(angles)) * factor


def exchange_kernel(loop_size, moves, order_hbm, spectra_hbm, assign_hbm, *refs):
    count = len(moves)
    same, own_same, kept, table = refs[:4]
    targets = refs[4 : 4 + count]
    sources = refs[4 + count : 4 + 2 * count]
    (
        order,
        spectra,
        assign,
        chunks,
        blocks,
        scratch,
        send_sems,
        recv_sems,
        go_sems,
        come_sems,
        in_sems,
    ) = refs[4 + 2 * count :]
    _, bins, _, rows, _ = chunks.shape
    half = rows // 2
    packed = 2 * bins
    width = 8 * rows
    quarter = loop_size // MEMBERS
    chan = lax.axis_index("chan")
    band = lax.axis_index("band")
    member = chan // quarter
    parity = lax.rem(member, 2)
    even = parity == 0
    swap = 1 - 2 * parity

    def device(distance, shift):
        where = lax.rem(chan + distance * quarter + loop_size, loop_size)
        return {"chan": where, "band": lax.rem(band + shift, 2)}

    def send(source, target, send_sem, recv_sem, where):
        return pltpu.make_async_remote_copy(
            src_ref=source,
            dst_ref=target,
            send_sem=send_sem,
            recv_sem=recv_sem,
            device_id=where,
            device_id_type=pl.DeviceIdType.MESH,
        )

    barrier = pltpu.get_barrier_semaphore()
    for distance in range(MEMBERS):
        for shift in range(2):
            if distance or shift:
                pl.semaphore_signal(
                    barrier,
                    inc=1,
                    device_id=device(distance, shift),
                    device_id_type=pl.DeviceIdType.MESH,
                )

    fetches = [
        pltpu.make_async_copy(order_hbm, order, in_sems.at[0]),
        pltpu.make_async_copy(spectra_hbm.at[0], spectra.at[0], in_sems.at[1]),
        pltpu.make_async_copy(spectra_hbm.at[1], spectra.at[1], in_sems.at[2]),
        pltpu.make_async_copy(assign_hbm, assign, in_sems.at[3]),
    ]
    for fetch in fetches:
        fetch.start()
    for fetch in fetches:
        fetch.wait()

    row_ids = lax.broadcasted_iota(jnp.int32, (rows, rows), 0)
    chosen = jnp.where(row_ids == order[...], 1.0, 0.0).astype(BF16)
    chosen = jnp.concatenate([chosen] * 3, axis=0)

    def arrange(which, slot):
        if which == MEMBERS:
            chunk = lax.rem(member + 3 - 2 * parity, MEMBERS)
        else:
            chunk = lax.rem(member + which, MEMBERS)
        for part in range(2):
            values = spectra[part, chunk * bins + slot]
            chunks[which, slot, part] = ordered_rows(chosen, values)

    forward = {}
    for slot in range(bins):
        for which in (2, 3, 1, MEMBERS):
            arrange(which, slot)
            landing = 0 if which == MEMBERS else MEMBERS - which
            at = slot * MEMBERS + landing
            forward[slot, landing] = send(
                chunks.at[which, slot],
                blocks.at[landing, slot],
                go_sems.at[at],
                come_sems.at[at],
                device(swap if which == MEMBERS else which, 0),
            )
        if slot == 0:
            pl.semaphore_wait(barrier, 2 * MEMBERS - 1)
        for landing in (2, 1, 3, 0):
            forward[slot, landing].start()

    def guarded(wanted, action):
        if wanted is None:
            action()
        else:
            pl.when(parity == wanted)(action)

    def start(at):
        distance, shift, wanted = moves[at]
        copy = send(
            sources[at], targets[at], send_sems.at[at], recv_sems.at[at], device(distance, shift)
        )
        guarded(wanted, copy.start)
        return copy

    def fill(out, row, lead, shift):
        first = lax.rem(band + shift, 2) * half
        for group in range(half // 8):
            out[row, :, group * width : (group + 1) * width] = (
                packed_rows(scratch, lead, first, rows, group, packed)
            )

    table[...] = lag_table(assign[...], member, band, bins, 1.0 / spectra.shape[3])
    returns = [None] * count
    for distance in range(MEMBERS):
        for slot in range(bins):
            if distance == 0:
                arrange(0, slot)
            real, imag = chunks[distance, slot, 0], chunks[distance, slot, 1]
            put_product(
                scratch,
                2 * MEMBERS + 1 + distance,
                slot,
                product(left_operand(real, imag), right_operand(real, imag)),
            )
        block = (MEMBERS - distance) % MEMBERS
        fill(same, block, 2 * MEMBERS + 1 + distance, 0)
        fill(sources[count - 1], block, 2 * MEMBERS + 1 + distance, 1)
    returns[count - 1] = start(count - 1)

    for slot in range(bins):
        for landing in (2, 1, 3, 0):
            forward[slot, landing].wait_recv()
        lefts, rights = [], []
        for at in range(MEMBERS):
            block = blocks if at else chunks
            real, imag = block[at, slot, 0], block[at, slot, 1]
            lefts.append(left_operand(real, imag))
            rights.append(right_operand(real, imag))
        for owner in (2, 1, 3, 0):
            for pair in range(2):
                partner = (owner + pair + 1) % MEMBERS
                put_product(scratch, owner * 2 + pair, slot, product(lefts[owner], rights[partner]))
        mine = [chunks[2, slot, part] for part in range(2)]
        theirs = [blocks[0, slot, part] for part in range(2)]
        first = [jnp.where(even, a, b) for a, b in zip(mine, theirs)]
        second = [jnp.where(even, b, a) for a, b in zip(mine, theirs)]
        put_product(
            scratch, 2 * MEMBERS, slot, product(left_operand(*first), right_operand(*second))
        )

    for at, (owner, shift, pairs) in enumerate(PIECES[:-1]):
        for row, pair in enumerate(pairs):
            fill(sources[at], row, owner * 2 + pair, shift)
        returns[at] = start(at)
    fill(own_same, 0, 2 * MEMBERS, 0)
    base = len(PIECES) - 1
    fill(sources[base], 0, 2 * MEMBERS, 0)
    returns[base] = start(base)
    fill(sources[base + 1], 0, 2 * MEMBERS, 1)
    fill(sources[base + 2], 0, 2 * MEMBERS, 1)
    returns[base + 1] = start(base + 1)
    returns[base + 2] = start(base + 2)
    for row, pair in enumerate(PIECES[-1][2]):
        fill(kept, row, pair, 0)

    for copy in forward.values():
        copy.wait_send()
    for copy, (distance, shift, wanted) in zip(returns, moves):
        guarded(wanted, copy.wait_send)
        guarded(None if wanted is None else (wanted + distance) % 2, copy.wait_recv)


def exchange(loop_size, order, spectra, assign):
    _, bins, rows, windows = spectra.shape
    bins = bins // MEMBERS
    columns = rows * rows // 2
    moves, leads = [], []
    for distance, shift, pairs in PIECES[:-1]:
        moves.append((distance, shift, (distance + 1) % 2 if pairs == (0,) else None))
        leads.append(len(pairs))
    moves += [(3, 0, 1), (3, 1, 1), (0, 1, 0), (0, 1, None)]
    leads += [1, 1, 1, MEMBERS]
    count = len(moves)
    outs = [(lead, 2 * bins, columns) for lead in [MEMBERS, 1, 2] + leads]
    outs.insert(3, (4 * MEMBERS * bins, 4 * MEMBERS * bins))
    results = pl.pallas_call(
        functools.partial(exchange_kernel, loop_size, moves),
        out_shape=tuple(jax.ShapeDtypeStruct(shape, F32) for shape in outs),
        in_specs=[HBM, HBM, HBM],
        out_specs=(VMEM,) * len(outs),
        scratch_shapes=[pltpu.VMEM((lead, 2 * bins, columns), F32) for lead in leads]
        + [
            pltpu.VMEM(order.shape, jnp.int32),
            pltpu.VMEM(spectra.shape, F32),
            pltpu.VMEM(assign.shape, jnp.int32),
            pltpu.VMEM((MEMBERS + 1, bins, 2, rows, windows), F32),
            pltpu.VMEM((MEMBERS, bins, 2, rows, windows), F32),
            pltpu.VMEM((3 * MEMBERS + 1, 2 * bins * rows, 128), F32),
            pltpu.SemaphoreType.DMA((count,)),
            pltpu.SemaphoreType.DMA((count,)),
            pltpu.SemaphoreType.DMA((bins * MEMBERS,)),
            pltpu.SemaphoreType.DMA((bins * MEMBERS,)),
            pltpu.SemaphoreType.DMA((4,)),
        ],
        compiler_params=pltpu.CompilerParams(
            collective_id=0, has_side_effects=True, vmem_limit_bytes=50 * 1024 * 1024
        ),
        name="exchange",
    )(order, spectra, assign)
    return results[:4], results[4:]


def lag_kernel(place, table, same, other, *refs):
    pieces, extras, written = refs[: len(PIECES)], refs[len(PIECES) : -3], refs[-3]
    out, sems = refs[-2:]
    columns = out.shape[2]
    tile = 640 if columns % 640 == 0 else columns
    high, low = halves(table[...])
    dims = ((1,), (0,))
    even = lax.rem(place[0], 2) == 0
    found = {}
    for piece, (distance, shift, pairs) in zip(pieces, PIECES):
        for row, pair in enumerate(pairs):
            found[pair, shift, distance] = piece, row
    own_same, own_other, theirs_same, theirs_other = extras
    more = {(1, 0): theirs_same, (1, 1): theirs_other, (2, 0): own_same, (2, 1): own_other}
    writes = []
    for pair in range(3):
        for at in range(0, columns, tile):
            span = slice(at, at + tile)
            if pair == 0:
                stacked = jnp.concatenate([same[:, span], other[:, span]], axis=0)
            else:
                terms = []
                for shift in range(2):
                    for distance in range(MEMBERS):
                        piece, row = found[pair - 1, shift, distance]
                        term = piece[row, :, span]
                        if pair == 1 and (distance, shift) in more:
                            term = jnp.where(even, more[distance, shift][0, :, span], term)
                        terms.append(term)
                stacked = jnp.concatenate(terms, axis=0)
            first, second = halves(stacked)
            out[pair, :, span] = dot(high, first, dims) + dot(high, second, dims) + dot(low, first, dims)
        write = pltpu.make_async_copy(out.at[pair], written.at[pair], sems.at[pair])
        write.start()
        writes.append(write)
    for write in writes:
        write.wait()


def lag_transform(place, table, same, other, pieces):
    lags = table.shape[0]
    columns = same.shape[1]
    return pl.pallas_call(
        lag_kernel,
        out_shape=jax.ShapeDtypeStruct((3, lags, columns), F32),
        in_specs=[SMEM] + [VMEM] * (3 + len(pieces)),
        out_specs=HBM,
        scratch_shapes=[pltpu.VMEM((3, lags, columns), F32), pltpu.SemaphoreType.DMA((3,))],
        compiler_params=pltpu.CompilerParams(vmem_limit_bytes=LIMIT),
        name="lag_transform",
    )(place, table, same, other, *pieces)


def on_device(loop_size, spectra, channel_order, bin_assign):
    member = lax.axis_index("chan") // (loop_size // MEMBERS)
    band = lax.axis_index("band")
    place = jnp.stack([member, band]).astype(jnp.int32)
    local, returned = exchange(loop_size, channel_order, spectra, bin_assign[None, :])
    same, own_same, kept, table = local
    *pieces, theirs_same, theirs_other, own_other, other = returned
    pieces += [kept, own_same, own_other, theirs_same, theirs_other]
    flat = (MEMBERS * same.shape[1], same.shape[2])
    return lag_transform(place, table, same.reshape(flat), other.reshape(flat), pieces)[None]


def solution(mesh):
    in_specs = (P(None, "band", ("grp", "chan"), None), P(("grp", "chan"), None), P())
    out_specs = P(("grp", "chan"), None, None, "band")
    return jax.shard_map(
        functools.partial(on_device, mesh.shape["chan"]),
        mesh=mesh,
        in_specs=in_specs,
        out_specs=out_specs,
        check_vma=False,
    )
```
